32 devices in a mesh: section: 4 (over x, core), ctx: 2 (over y), tp: 4 (over z).
Axes of the slice: x: 2, y: 2, z: 4, core: 2. Of those that a mesh axis runs over, the one named last changes fastest.
Arguments:
- mixer_input: bfloat16 [4, 1024, 8192], P('section', 'ctx', 'tp'), may hold values from -6 to 6
- write_vectors: bfloat16 [4, 1024, 1024], P('section', 'ctx', 'tp'), may hold values from -6 to 6
- read_vectors: bfloat16 [4, 1024, 1024], P('section', 'ctx', 'tp'), may hold values from -6 to 6
- delta_raw: float32 [4, 1024, 128], P('section', 'ctx', 'tp'), as said below
- log_rates: float32 [4, 128], P('section', 'tp'), as said below
- delta_bias: float32 [4, 128], P('section', 'tp'), as said below
- skip_gain: float32 [4, 128], P('section', 'tp'), may hold values from 0.5 to 1.5
- output_grad: bfloat16 [4, 1024, 8192], P('section', 'ctx', 'tp'), may hold values from -6 to 6
Outputs:
- upstream_grad: bfloat16 [4, 1024, 8192], P('section', 'ctx', 'tp')
- grad_delta: float32 [4, 1024, 128], P('section', 'ctx', 'tp')
- grad_vectors: float32 [4, 1024, 2048], P('section', ('ctx', 'tp'))
- grad_params: float32 [4, 3, 128], P('section', None, 'tp')
The draws below stay inside these ranges and needn't reach their ends.
Inputs may be any that keep to these rules, and one draw needn't show every extreme that they name: `log_rates`: one value a head and section. `delta_bias`: one value a head and section. `delta_raw`: real-valued logits.
All inputs are finite; a program needn't handle non-finite values.
Results may differ from the reference program's by a relative error of at most 0.00365.
Values may be sent and summed in bfloat16 or wider, within the bound.
A program may use at most 128 MiB of HBM per device.

```python
import jax
import jax.numpy as jnp
from jax import lax

HEADS = 128
HEADDIM = 64
STATE = 128
GROUPS = 8
BLOCK = 256
TOK_DEV = 512
TOKENS = 1024
SECTIONS = 4


def head_table(key):
    class_key = jax.random.fold_in(key, 101)
    level_key = jax.random.fold_in(key, 102)
    rate_key = jax.random.fold_in(key, 103)
    share = 0.5
    fast_heads = jax.random.uniform(class_key, (SECTIONS, HEADS), jnp.float32) < share
    level = jnp.exp(jax.random.uniform(level_key, (SECTIONS, HEADS), jnp.float32, -0.2, 0.2))
    slow_step = level / jnp.sqrt(STATE * TOKENS * 1.0)
    fast_step = 0.16 * level / jnp.sqrt(STATE * 1.0)
    base_step = jnp.where(fast_heads, fast_step, slow_step)
    spread = jax.random.uniform(rate_key, (SECTIONS, HEADS), jnp.float32, 0.0, 1.0)
    fast_rate = jnp.exp(0.25 * (2.0 * spread - 1.0)) / (40.0 * base_step)
    slow_rate = (0.3 + 0.5 * spread) / (TOKENS * base_step)
    return (base_step, jnp.where(fast_heads, fast_rate, slow_rate))


def draw_log_rates(key, part):
    base_step, rates = head_table(key)
    return jnp.log(rates)


def draw_delta_bias(key, part):
    base_step, rates = head_table(key)
    return jnp.log(jnp.expm1(base_step))


def draw_delta_raw(key, part):
    noise_key = jax.random.fold_in(key, 3)
    shift_key = jax.random.fold_in(key, 5)
    noise = 0.5 * jax.random.truncated_normal(noise_key, -2.5, 2.5, (SECTIONS, TOKENS, HEADS), jnp.float32)
    block_count = TOKENS // TOK_DEV
    offset = jax.random.uniform(shift_key, (SECTIONS, block_count, 1, HEADS), jnp.float32, -8.0, 0.7)
    offset = jnp.broadcast_to(offset, (SECTIONS, block_count, TOK_DEV, HEADS)).reshape(SECTIONS, TOKENS, HEADS)
    return noise + offset


def shard_levels(stream_key, dims, pieces, least, top_value):
    gain = 1.0
    for position, blocks in pieces:
        steps = jax.random.uniform(jax.random.fold_in(jax.random.fold_in(stream_key, 6), position), (blocks,), jnp.float32, least / len(pieces), top_value / len(pieces))
        gain = gain * jnp.repeat(jnp.exp(steps), dims[position] // blocks).reshape((-1,) + (1,) * (len(dims) - 1 - position))
    return gain


def gaussian(stream_key, dims, width, reach, pieces=(), dtype=jnp.bfloat16):
    result = jax.random.normal(stream_key, dims, jnp.float32) * width
    if len(pieces) > 0:
        result = shard_levels(stream_key, dims, pieces, -0.22, 0.18) * result
    return jnp.clip(result, min=-reach, max=reach).astype(dtype)


def setup_inputs(seed: int = 0) -> dict:
    seeds = jax.random.split(jax.random.key(seed), 9)
    return {
        "mixer_input": gaussian(seeds[0], (SECTIONS, TOKENS, HEADS * HEADDIM), 1.0, 6.0, ((0, 4), (1, 2), (2, 4))),
        "write_vectors": gaussian(seeds[1], (SECTIONS, TOKENS, GROUPS * STATE), 1.0, 6.0, ((0, 4), (1, 2), (2, 4))),
        "read_vectors": gaussian(seeds[2], (SECTIONS, TOKENS, GROUPS * STATE), 1.0, 6.0, ((0, 4), (1, 2), (2, 4))),
        "delta_raw": draw_delta_raw(jax.random.fold_in(seeds[8], 71), 0),
        "log_rates": draw_log_rates(jax.random.fold_in(seeds[8], 71), 0),
        "delta_bias": draw_delta_bias(jax.random.fold_in(seeds[8], 71), 0),
        "skip_gain": jnp.clip(0.5 + 1.0 * jax.random.uniform(seeds[6], (SECTIONS, HEADS), jnp.float32) ** shard_levels(seeds[6], (SECTIONS, HEADS), ((0, 4), (1, 4)), -0.2, 0.2), 0.5, 1.5),
        "output_grad": gaussian(seeds[7], (SECTIONS, TOKENS, HEADS * HEADDIM), 1.0, 6.0, ((0, 4), (1, 2), (2, 4))),
    }


HIGHEST = lax.Precision.HIGHEST

def block_pass(values_all, write_rows, read_rows, step_size, decay_rates, start_state):
    length, group_count, per_group, head_width = values_all.shape
    block_count = length // BLOCK
    positions = jnp.arange(BLOCK)
    causal = positions[:, None] >= positions[None, :]

    def advance(carry_state, block_item):
        values, write_block, read_block, step_rows = block_item
        cum_log = jnp.cumsum(-step_rows * decay_rates[None], axis=0)
        gap_logs = cum_log[:, None] - cum_log[None, :]
        decay_mat = jnp.exp(jnp.where(causal[:, :, None, None], gap_logs, -1e+30))
        scores = jnp.einsum('ign,jgn->ijg', read_block, write_block, precision=HIGHEST)
        weights = scores[:, :, :, None] * decay_mat * step_rows[None]
        within = jnp.einsum('ijgk,jgkp->igkp', weights, values, precision=HIGHEST)
        carried = jnp.einsum('ign,gkpn->igkp', read_block, carry_state, precision=HIGHEST)
        outputs = within + jnp.exp(cum_log)[..., None] * carried
        tail_w = jnp.exp(cum_log[-1][None] - cum_log) * step_rows
        written = jnp.einsum('jgkp,jgn->gkpn', tail_w[..., None] * values, write_block, precision=HIGHEST)
        new_state = jnp.exp(cum_log[-1])[..., None, None] * carry_state + written
        return (new_state, outputs)
    blocks_in = (values_all.reshape(block_count, BLOCK, group_count, per_group, head_width), write_rows.reshape(block_count, BLOCK, group_count, -1), read_rows.reshape(block_count, BLOCK, group_count, -1), step_size.reshape(block_count, BLOCK, group_count, per_group))
    last_state, outputs = lax.scan(jax.checkpoint(advance), start_state, blocks_in)
    return (outputs.reshape(length, group_count, per_group, head_width), last_state)

def layer_output(input_rows, write_rows, read_rows, delta_rows, rate_logs, bias_terms, skip_terms):
    length = input_rows.shape[0]
    group_count = write_rows.shape[1] // STATE
    head_count = rate_logs.shape[0]
    per_group = head_count // group_count
    step_size = jax.nn.softplus(delta_rows + bias_terms[None, :]).reshape(length, group_count, per_group)
    decay_rates = jnp.exp(rate_logs).reshape(group_count, per_group)
    values = input_rows.reshape(length, group_count, per_group, HEADDIM)
    start_state = jnp.zeros((group_count, per_group, HEADDIM, STATE), jnp.float32)
    outputs, unused = block_pass(values, write_rows.reshape(length, group_count, STATE), read_rows.reshape(length, group_count, STATE), step_size, decay_rates, start_state)
    outputs = outputs + skip_terms.reshape(group_count, per_group)[None, :, :, None] * values
    return outputs.reshape(input_rows.shape)

def reference(mixer_input, write_vectors, read_vectors, delta_raw, log_rates, delta_bias, skip_gain, output_grad):

    def one_section(section_items):
        input_rows, write_rows, read_rows, delta_rows, rate_logs, bias_terms, skip_terms, grad_rows = section_items
        unused, pullback = jax.vjp(layer_output, input_rows.astype(jnp.float32), write_rows.astype(jnp.float32), read_rows.astype(jnp.float32), delta_rows, rate_logs, bias_terms, skip_terms)
        return pullback(grad_rows.astype(jnp.float32))
    gradients = lax.map(one_section, (mixer_input, write_vectors, read_vectors, delta_raw, log_rates, delta_bias, skip_gain, output_grad))
    grad_input = gradients[0].astype(jnp.bfloat16)
    upstream = jnp.concatenate([grad_input[1:], jnp.zeros_like(grad_input[:1])], axis=0)
    section_count = gradients[1].shape[0]
    length = gradients[1].shape[1]
    grad_write = gradients[1].reshape(section_count, length, GROUPS, STATE)
    grad_read = gradients[2].reshape(section_count, length, GROUPS, STATE)
    grad_vectors = jnp.stack([grad_write, grad_read], axis=3).reshape(section_count, length, GROUPS * 2 * STATE)
    grad_params = jnp.stack([gradients[4], gradients[5], gradients[6]], axis=1)
    return (upstream, gradients[3], grad_vectors, grad_params)
```

```python
import functools
import math

import jax
import jax.numpy as jnp
from jax import lax
from jax.experimental import pallas as pl
from jax.experimental.pallas import tpu as pltpu
from jax.sharding import PartitionSpec as P

HEADDIM = 64
STATE = 128
LANES = 128
LOG2E = math.log2(math.e)
MESH = pl.DeviceIdType.MESH
HIGHEST = lax.Precision.HIGHEST
F32 = jnp.float32
BF16 = jnp.bfloat16


def dot_nn(a, b, precision=None):
    return lax.dot_general(
        a, b, (((1,), (0,)), ((), ())), precision=precision, preferred_element_type=F32
    )


def dot_nt(a, b):
    return lax.dot_general(a, b, (((1,), (1,)), ((), ())), preferred_element_type=F32)


def dot_tn(a, b):
    return lax.dot_general(a, b, (((0,), (0,)), ((), ())), preferred_element_type=F32)


def kernel(
    sizes,
    x_ref,
    w_ref,
    r_ref,
    delta_ref,
    rates_ref,
    bias_ref,
    skip_ref,
    dy_ref,
    up_ref,
    gdelta_ref,
    vec_ref,
    params_ref,
    cum,
    cum_rows,
    step_rows,
    tail,
    decay,
    ratio,
    slope,
    lead_wide,
    tail_wide,
    lead_dy,
    tail_x,
    states,
    exits,
    state_in,
    state_out,
    exit_in,
    exit_out,
    read_state,
    write_exit,
    da,
    pieces,
    edge,
    dx,
    vec_out,
    vec_in,
    part,
    parts,
    s_send,
    s_recv,
    e_send,
    e_recv,
    x_send,
    x_recv,
    v_send,
    v_recv,
    p_send,
    p_recv,
):
    sections, ctxs, tps = sizes
    section, ctx, tp = (lax.axis_index(a) for a in ("section", "ctx", "tp"))
    length, heads = delta_ref.shape
    groups = w_ref.shape[1] // STATE
    per_group = heads // groups
    width = per_group * HEADDIM
    chunk = length // tps
    chunks = tps
    pairs = width // LANES

    barrier = pltpu.get_barrier_semaphore()
    for hop in range(1, ctxs):
        pl.semaphore_signal(
            barrier, inc=1, device_id={"ctx": lax.rem(ctx + hop, ctxs)}, device_id_type=MESH
        )
    for hop in range(1, tps):
        pl.semaphore_signal(
            barrier, inc=1, device_id={"tp": lax.rem(tp + hop, tps)}, device_id_type=MESH
        )

    @pl.when(section > 0)
    def _():
        pl.semaphore_signal(barrier, inc=1, device_id={"section": section - 1}, device_id_type=MESH)

    @pl.when(section < sections - 1)
    def _():
        pl.semaphore_signal(barrier, inc=1, device_id={"section": section + 1}, device_id_type=MESH)

    up_to = lax.broadcasted_iota(jnp.int32, (chunk, chunk), 0)
    from_ = lax.broadcasted_iota(jnp.int32, (chunk, chunk), 1)
    causal = up_to >= from_
    lower = causal.astype(F32)
    upper = (up_to <= from_).astype(F32)
    first_half = lax.broadcasted_iota(jnp.int32, (chunk, LANES), 1) < HEADDIM
    rate = jnp.exp(rates_ref[...])
    for k in range(chunks):
        rows = slice(k * chunk, (k + 1) * chunk)
        z = delta_ref[rows, :] + bias_ref[...]
        small = jnp.exp(-jnp.abs(z))
        step = jnp.maximum(z, 0.0) + jnp.log1p(small)
        sig = jnp.where(z >= 0, 1.0, small) / (1.0 + small)
        dec = -step * rate
        decay[rows, :] = dec
        ratio[rows, :] = jnp.where(step > 1e-37, sig / jnp.maximum(step, 1e-37), 1.0)
        slope[rows, :] = sig * rate
        run = dot_nn(lower, dec * LOG2E, HIGHEST)
        cum[rows, :] = run
        tail[rows, :] = jnp.exp2(run[chunk - 1 : chunk, :] - run) * step
        cum_rows[:, rows] = jnp.transpose(run)
        step_rows[:, rows] = jnp.transpose(step)

    def entered():
        peers = (ctxs - 1) + (tps - 1)
        peers = peers + jnp.where(section > 0, 1, 0) + jnp.where(section < sections - 1, 1, 0)
        pl.semaphore_wait(barrier, peers)

    def columns(g, j):
        start = g * width + j * LANES
        return slice(start, start + LANES)

    def spread(ref, rows, head):
        both = ref[rows, head : head + 2]
        return jnp.where(
            first_half,
            jnp.broadcast_to(both[:, 0:1], (chunk, LANES)),
            jnp.broadcast_to(both[:, 1:2], (chunk, LANES)),
        )

    def increments(g):
        def one(k, carry):
            rows = pl.ds(pl.multiple_of(k * chunk, chunk), chunk)
            for j in range(pairs):
                at = columns(g, j)
                head = g * per_group + 2 * j
                lead_pair = jnp.exp2(spread(cum, rows, head))
                tail_pair = spread(tail, rows, head)
                lead_wide[rows, at] = lead_pair
                tail_wide[rows, at] = tail_pair
                lead_dy[rows, at] = (lead_pair * dy_ref[rows, at].astype(F32)).astype(BF16)
                tail_x[rows, at] = (tail_pair * x_ref[rows, at].astype(F32)).astype(BF16)
            group_at = slice(g * width, (g + 1) * width)
            vec_at = slice(g * STATE, (g + 1) * STATE)
            states[g, k] = dot_tn(w_ref[rows, vec_at], tail_x[rows, group_at])
            exits[g, k] = dot_tn(r_ref[rows, vec_at], lead_dy[rows, group_at])
            return carry

        lax.fori_loop(0, chunks, one, 0)

    def last_row(g, k, j):
        row = (k + 1) * chunk - 1
        return lead_wide[row : row + 1, columns(g, j)]

    def scan_states(g, first):
        for j in range(pairs):
            at = slice(j * LANES, (j + 1) * LANES)
            now = jnp.zeros((STATE, LANES), F32) if first else state_in[g, :, at].astype(F32)
            for k in range(chunks):
                new = states[g, k, :, at]
                states[g, k, :, at] = now
                now = last_row(g, k, j) * now + new
            states[g, chunks, :, at] = now
            state_out[g, :, at] = now.astype(BF16)

    def scan_exits(g, first):
        for j in range(pairs):
            at = slice(j * LANES, (j + 1) * LANES)
            now = jnp.zeros((STATE, LANES), F32) if first else exit_in[g, :, at].astype(F32)
            for k in reversed(range(chunks)):
                new = exits[g, k, :, at]
                exits[g, k, :, at] = now
                now = last_row(g, k, j) * now + new
            exit_out[g, :, at] = now.astype(BF16)

    def state_copy(g):
        return pltpu.make_async_remote_copy(
            src_ref=state_out.at[g],
            dst_ref=state_in.at[g],
            send_sem=s_send.at[g],
            recv_sem=s_recv.at[g],
            device_id={"ctx": jnp.minimum(ctx + 1, ctxs - 1)},
            device_id_type=MESH,
        )

    def exit_copy(g):
        return pltpu.make_async_remote_copy(
            src_ref=exit_out.at[g],
            dst_ref=exit_in.at[g],
            send_sem=e_send.at[g],
            recv_sem=e_recv.at[g],
            device_id={"ctx": jnp.maximum(ctx - 1, 0)},
            device_id_type=MESH,
        )

    def begin(g):
        @pl.when(ctx == 0)
        def _():
            scan_states(g, True)
            if ctxs > 1:
                state_copy(g).start()

        @pl.when(ctx == ctxs - 1)
        def _():
            scan_exits(g, True)
            if ctxs > 1:
                exit_copy(g).start()

    def link(g):
        @pl.when(ctx > 0)
        def _():
            state_copy(g).wait_recv()
            scan_states(g, False)

        if ctxs > 2:

            @pl.when((ctx > 0) & (ctx < ctxs - 1))
            def _():
                state_copy(g).start()

        @pl.when(ctx < ctxs - 1)
        def _():
            exit_copy(g).wait_recv()
            scan_exits(g, False)

        if ctxs > 2:

            @pl.when((ctx > 0) & (ctx < ctxs - 1))
            def _():
                exit_copy(g).start()

    def dx_copy(g, k):
        rows = pl.ds(pl.multiple_of(k * chunk, chunk), chunk)
        at = pl.ds(g * width, width)
        return pltpu.make_async_remote_copy(
            src_ref=dx.at[rows, at],
            dst_ref=up_ref.at[rows, at],
            send_sem=x_send.at[g, k],
            recv_sem=x_recv.at[g, k],
            device_id={"section": jnp.maximum(section - 1, 0)},
            device_id_type=MESH,
        )

    def vec_copy(g, k):
        return pltpu.make_async_remote_copy(
            src_ref=vec_out.at[g, k],
            dst_ref=vec_in.at[g, tp],
            send_sem=v_send.at[g, k],
            recv_sem=v_recv.at[g, tp],
            device_id={"tp": k},
            device_id_type=MESH,
        )

    def vec_arrival(g, k):
        return pltpu.make_async_remote_copy(
            src_ref=vec_out.at[g, k],
            dst_ref=vec_in.at[g, k],
            send_sem=v_send.at[g, k],
            recv_sem=v_recv.at[g, k],
            device_id={"tp": k},
            device_id_type=MESH,
        )

    def quadratic(g):
        vec_at = slice(g * STATE, (g + 1) * STATE)
        group_at = slice(g * width, (g + 1) * width)
        gather = (
            lax.broadcasted_iota(jnp.int32, (width, heads), 0) // HEADDIM + g * per_group
            == lax.broadcasted_iota(jnp.int32, (width, heads), 1)
        ).astype(F32)
        gather_short = gather.astype(BF16)

        def one(k, carry):
            rows = pl.ds(pl.multiple_of(k * chunk, chunk), chunk)
            w, r = w_ref[rows, vec_at], r_ref[rows, vec_at]
            scores = jnp.where(causal, dot_nt(r, w), 0.0)
            da[...] = jnp.zeros_like(da)
            state, exit_ = states[g, k].astype(BF16), exits[g, k].astype(BF16)
            read_state[...] = dot_nn(r, state)
            write_exit[...] = dot_nn(w, exit_)
            edge[0:1, :] = jnp.sum(exits[g, k] * states[g, k + 1], axis=0, keepdims=True)
            for j in range(pairs):
                at = columns(g, j)
                here = slice(j * LANES, (j + 1) * LANES)
                head = g * per_group + 2 * j
                xs, dys = x_ref[rows, at], dy_ref[rows, at]
                none = jnp.zeros_like(xs)
                x_split = jnp.concatenate(
                    [jnp.where(first_half, xs, none), jnp.where(first_half, none, xs)], axis=0
                )
                dy_split = jnp.concatenate(
                    [jnp.where(first_half, dys, none), jnp.where(first_half, none, dys)], axis=0
                )
                product = dot_nt(dy_split, xs)
                weights = []
                total = da[...]
                for u in range(2):
                    one_head = head + u
                    gap = cum[rows, one_head : one_head + 1] - cum_rows[one_head : one_head + 1, rows]
                    kept = jnp.exp2(jnp.minimum(gap, 0.0)) * step_rows[one_head : one_head + 1, rows]
                    weights.append((kept * scores).astype(BF16))
                    total = total + kept * product[u * chunk : (u + 1) * chunk]
                da[...] = total
                y = dot_nn(jnp.concatenate(weights, axis=1), x_split)
                y = y + lead_wide[rows, at] * read_state[:, here]
                dxs = dot_tn(jnp.concatenate(weights, axis=0), dy_split)
                dxs = dxs + tail_wide[rows, at] * write_exit[:, here]
                x32, dy32 = xs.astype(F32), dys.astype(F32)
                column = x32 * dxs
                rest = dy32 * y - column
                high = rest.astype(BF16)
                pieces[0:chunk, here] = high
                pieces[chunk : 2 * chunk, here] = (rest - high.astype(F32)).astype(BF16)
                pieces[2 * chunk : 3 * chunk, here] = column.astype(BF16)
                edge[1:2, here] = jnp.sum(x32 * dy32, axis=0, keepdims=True)
                gain = jnp.where(
                    first_half[0:1],
                    jnp.broadcast_to(skip_ref[:, head : head + 1], (1, LANES)),
                    jnp.broadcast_to(skip_ref[:, head + 1 : head + 2], (1, LANES)),
                )
                dx[rows, at] = (dxs + gain * dy32).astype(BF16)

            @pl.when(section > 0)
            def _():
                dx_copy(g, k).start()

            inner = jnp.where(causal, da[...], 0.0).astype(BF16)
            dw = dot_tn(inner, r) + dot_nt(tail_x[rows, group_at], exit_)
            dr = dot_nn(inner, w) + dot_nt(lead_dy[rows, group_at], state)

            @pl.when(tp == k)
            def _():
                vec_in[g, k, :, 0:STATE] = dw.astype(BF16)
                vec_in[g, k, :, STATE : 2 * STATE] = dr.astype(BF16)

            @pl.when(tp != k)
            def _():
                vec_out[g, k, :, 0:STATE] = dw.astype(BF16)
                vec_out[g, k, :, STATE : 2 * STATE] = dr.astype(BF16)
                vec_copy(g, k).start()

            sums = dot_nn(pieces[...], gather_short)
            ends = dot_nn(edge[...], gather, HIGHEST)
            difference = sums[0:chunk] + sums[chunk : 2 * chunk]
            decay_grad = dot_nn(upper, difference, HIGHEST) + ends[0:1]
            grad = sums[2 * chunk : 3 * chunk] * ratio[rows, :] - decay_grad * slope[rows, :]
            mine = lax.broadcasted_iota(jnp.int32, (chunk, heads), 1) // per_group == g
            grad = jnp.where(mine, grad, 0.0)
            if g == 0:
                gdelta_ref[rows, :] = grad
            else:
                gdelta_ref[rows, :] += grad
            part[0:1, 0:heads] += jnp.sum(decay_grad * decay[rows, :], axis=0, keepdims=True)
            part[1:2, 0:heads] += jnp.sum(grad, axis=0, keepdims=True)
            part[2:3, 0:heads] += ends[1:2]
            return carry

        lax.fori_loop(0, chunks, one, 0)

    part[...] = jnp.zeros_like(part)
    edge[...] = jnp.zeros_like(edge)
    for g in range(groups):
        increments(g)
        if g == 0:
            entered()
        begin(g)
    for g in range(groups):
        link(g)
        quadratic(g)

    def part_copy(hop):
        other = lax.rem(ctx + hop, ctxs)
        return pltpu.make_async_remote_copy(
            src_ref=part,
            dst_ref=parts.at[hop - 1],
            send_sem=p_send.at[hop - 1],
            recv_sem=p_recv.at[hop - 1],
            device_id={"ctx": other},
            device_id_type=MESH,
        )

    for hop in range(1, ctxs):
        part_copy(hop).start()
    for g in range(groups):

        @pl.when(ctx < ctxs - 1)
        def _():
            state_copy(g).wait_send()

        @pl.when(ctx > 0)
        def _():
            exit_copy(g).wait_send()

        def vectors(k, carry):
            @pl.when(tp != k)
            def _():
                vec_arrival(g, k).wait_recv()
                vec_arrival(g, k).wait_send()

            return carry

        lax.fori_loop(0, tps, vectors, 0)
        for k in range(tps):
            start = (k * groups + g) * 2 * STATE
            vec_ref[:, start : start + 2 * STATE] = vec_in[g, k].astype(F32)
    result = part[...]
    for hop in range(1, ctxs):
        part_copy(hop).wait()
        result = result + parts[hop - 1]
    params_ref[...] = result[0:3, 0:heads]
    for g in range(groups):

        def moved(k, carry):
            @pl.when(section > 0)
            def _():
                dx_copy(g, k).wait_send()

            @pl.when(section < sections - 1)
            def _():
                dx_copy(g, k).wait_recv()

            return carry

        lax.fori_loop(0, chunks, moved, 0)


def shards(
    sizes,
    mixer_input,
    write_vectors,
    read_vectors,
    delta_raw,
    log_rates,
    delta_bias,
    skip_gain,
    output_grad,
):
    sections, ctxs, tps = sizes
    length, heads = delta_raw.shape[1:]
    columns = mixer_input.shape[2]
    groups = write_vectors.shape[2] // STATE
    width = columns // groups
    chunk = length // tps
    dma = pltpu.SemaphoreType.DMA
    vmem = pltpu.VMEM
    scratch = [
        vmem((length, heads), F32),
        vmem((heads, length), F32),
        vmem((heads, length), F32),
        vmem((length, heads), F32),
        vmem((length, heads), F32),
        vmem((length, heads), F32),
        vmem((length, heads), F32),
        vmem((length, columns), F32),
        vmem((length, columns), F32),
        vmem((length, columns), BF16),
        vmem((length, columns), BF16),
        vmem((groups, tps + 1, STATE, width), F32),
        vmem((groups, tps, STATE, width), F32),
        vmem((groups, STATE, width), BF16),
        vmem((groups, STATE, width), BF16),
        vmem((groups, STATE, width), BF16),
        vmem((groups, STATE, width), BF16),
        vmem((chunk, width), F32),
        vmem((chunk, width), F32),
        vmem((chunk, chunk), F32),
        vmem((3 * chunk, width), BF16),
        vmem((8, width), F32),
        vmem((length, columns), BF16),
        vmem((groups, tps, chunk, 2 * STATE), BF16),
        vmem((groups, tps, chunk, 2 * STATE), BF16),
        vmem((8, LANES), F32),
        vmem((max(ctxs - 1, 1), 8, LANES), F32),
        dma((groups,)),
        dma((groups,)),
        dma((groups,)),
        dma((groups,)),
        dma((groups, tps)),
        dma((groups, tps)),
        dma((groups, tps)),
        dma((groups, tps)),
        dma((max(ctxs - 1, 1),)),
        dma((max(ctxs - 1, 1),)),
    ]
    whole = pl.BlockSpec(memory_space=pltpu.VMEM)
    upstream, grad_delta, vectors, params = pl.pallas_call(
        functools.partial(kernel, sizes),
        out_shape=(
            jax.ShapeDtypeStruct((length, columns), BF16),
            jax.ShapeDtypeStruct((length, heads), F32),
            jax.ShapeDtypeStruct((chunk, groups * tps * 2 * STATE), F32),
            jax.ShapeDtypeStruct((3, heads), F32),
        ),
        in_specs=[whole] * 8,
        out_specs=(pl.BlockSpec(memory_space=pl.ANY), whole, whole, whole),
        scratch_shapes=scratch,
        compiler_params=pltpu.CompilerParams(
            collective_id=0, has_side_effects=True, vmem_limit_bytes=56 * 1024 * 1024
        ),
    )(
        mixer_input[0],
        write_vectors[0],
        read_vectors[0],
        delta_raw[0],
        log_rates,
        delta_bias,
        skip_gain,
        output_grad[0],
    )
    last = lax.axis_index("section") == sections - 1
    upstream = jnp.where(last, jnp.zeros_like(upstream), upstream)
    return (upstream[None], grad_delta[None], vectors[None], params[None])


def solution(mesh):
    sizes = tuple(mesh.shape[a] for a in ("section", "ctx", "tp"))
    in_specs = (
        P("section", "ctx", "tp"),
        P("section", "ctx", "tp"),
        P("section", "ctx", "tp"),
        P("section", "ctx", "tp"),
        P("section", "tp"),
        P("section", "tp"),
        P("section", "tp"),
        P("section", "ctx", "tp"),
    )
    out_specs = (
        P("section", "ctx", "tp"),
        P("section", "ctx", "tp"),
        P("section", ("ctx", "tp"), None),
        P("section", None, "tp"),
    )
    return jax.shard_map(
        functools.partial(shards, sizes),
        mesh=mesh,
        in_specs=in_specs,
        out_specs=out_specs,
        check_vma=False,
    )
```

```python
import functools
import math

import jax
import jax.numpy as jnp
from jax import lax
from jax.experimental import pallas as pl
from jax.experimental.pallas import tpu as pltpu
from jax.sharding import PartitionSpec as P

HEADDIM = 64
STATE = 128
LANES = 128
LOG2E = math.log2(math.e)
MESH = pl.DeviceIdType.MESH
HIGHEST = lax.Precision.HIGHEST
F32 = jnp.float32
BF16 = jnp.bfloat16


def dot_nn(a, b, precision=None):
    return lax.dot_general(
        a, b, (((1,), (0,)), ((), ())), precision=precision, preferred_element_type=F32
    )


def dot_nt(a, b):
    return lax.dot_general(a, b, (((1,), (1,)), ((), ())), preferred_element_type=F32)


def dot_tn(a, b):
    return lax.dot_general(a, b, (((0,), (0,)), ((), ())), preferred_element_type=F32)


def split(a, parts):
    out = []
    for _ in range(parts):
        out.append(a.astype(BF16))
        a = a - out[-1].astype(F32)
    return out


def dot_exact(a, b):
    rows = a.shape[0]
    terms = dot_nn(jnp.concatenate(split(a, 3), axis=0), b)
    return terms[0:rows] + terms[rows : 2 * rows] + terms[2 * rows : 3 * rows]


def kernel(
    sizes,
    x_ref,
    w_ref,
    r_ref,
    delta_ref,
    rates_ref,
    bias_ref,
    skip_ref,
    dy_ref,
    up_ref,
    gdelta_ref,
    vec_ref,
    params_ref,
    cum,
    cum_rows,
    step_rows,
    scales,
    decay,
    ratio,
    slope,
    lead_wide,
    tail_wide,
    lead_dy,
    tail_x,
    states,
    exits,
    state_in,
    state_out,
    exit_in,
    exit_out,
    read_state,
    write_exit,
    da,
    pieces,
    edge,
    dx,
    vec_out,
    vec_in,
    part,
    parts,
    s_send,
    s_recv,
    e_send,
    e_recv,
    x_send,
    x_recv,
    v_send,
    v_recv,
    p_send,
    p_recv,
):
    sections, ctxs, tps = sizes
    section, ctx, tp = (lax.axis_index(a) for a in ("section", "ctx", "tp"))
    heads, length = delta_ref.shape
    groups = w_ref.shape[1] // STATE
    per_group = heads // groups
    width = per_group * HEADDIM
    chunk = length // tps
    chunks = tps
    pairs = width // LANES

    barrier = pltpu.get_barrier_semaphore()
    for hop in range(1, ctxs):
        pl.semaphore_signal(
            barrier, inc=1, device_id={"ctx": lax.rem(ctx + hop, ctxs)}, device_id_type=MESH
        )
    for hop in range(1, tps):
        pl.semaphore_signal(
            barrier, inc=1, device_id={"tp": lax.rem(tp + hop, tps)}, device_id_type=MESH
        )

    @pl.when(section > 0)
    def _():
        pl.semaphore_signal(barrier, inc=1, device_id={"section": section - 1}, device_id_type=MESH)

    @pl.when(section < sections - 1)
    def _():
        pl.semaphore_signal(barrier, inc=1, device_id={"section": section + 1}, device_id_type=MESH)

    up_to = lax.broadcasted_iota(jnp.int32, (chunk, chunk), 0)
    from_ = lax.broadcasted_iota(jnp.int32, (chunk, chunk), 1)
    causal = up_to >= from_
    lower = causal.astype(BF16)
    upper = (up_to <= from_).astype(BF16)
    first_half = lax.broadcasted_iota(jnp.int32, (chunk, LANES), 1) < HEADDIM
    rate = jnp.transpose(jnp.broadcast_to(jnp.exp(rates_ref[...]), (chunk, heads)))
    bias = jnp.transpose(jnp.broadcast_to(bias_ref[...], (chunk, heads)))
    for k in range(chunks):
        rows = slice(k * chunk, (k + 1) * chunk)
        z = delta_ref[:, rows] + bias
        small = jnp.exp(-jnp.abs(z))
        step = jnp.maximum(z, 0.0) + jnp.log1p(small)
        sig = jnp.where(z >= 0, 1.0, small) / (1.0 + small)
        dec = -step * rate
        decay[:, rows] = dec
        ratio[:, rows] = jnp.where(step > 1e-37, sig / jnp.maximum(step, 1e-37), 1.0)
        slope[:, rows] = sig * rate
        run = dot_exact(dec * LOG2E, upper)
        cum[rows, :] = jnp.transpose(run)
        cum_rows[:, rows] = run
        step_rows[:, rows] = step
        lead = split(jnp.exp2(run), 2)
        tail = split(jnp.exp2(run[:, chunk - 1 : chunk] - run) * step, 2)
        for g in range(groups):
            own = slice(g * per_group, (g + 1) * per_group)
            scales[g, 0, :, rows] = jnp.concatenate([lead[0][own], lead[1][own]], axis=0)
            scales[g, 1, :, rows] = jnp.concatenate([tail[0][own], tail[1][own]], axis=0)
    head_of = lax.broadcasted_iota(jnp.int32, (2 * per_group, width), 1) // HEADDIM
    row_of = lax.broadcasted_iota(jnp.int32, (2 * per_group, width), 0)
    both = (head_of == lax.rem(row_of, per_group)).astype(BF16)
    gather = both[0:per_group]

    def entered():
        peers = (ctxs - 1) + (tps - 1)
        peers = peers + jnp.where(section > 0, 1, 0) + jnp.where(section < sections - 1, 1, 0)
        pl.semaphore_wait(barrier, peers)

    def columns(g, j):
        start = g * width + j * LANES
        return slice(start, start + LANES)

    def increments(g):
        def one(k, carry):
            rows = pl.ds(pl.multiple_of(k * chunk, chunk), chunk)
            group_at = slice(g * width, (g + 1) * width)
            vec_at = slice(g * STATE, (g + 1) * STATE)
            lead_all = dot_tn(scales[g, 0, :, rows], both)
            tail_all = dot_tn(scales[g, 1, :, rows], both)
            lead_wide[rows, group_at] = lead_all
            tail_wide[rows, group_at] = tail_all
            lead_dy[rows, group_at] = (lead_all * dy_ref[rows, group_at].astype(F32)).astype(BF16)
            tail_x[rows, group_at] = (tail_all * x_ref[rows, group_at].astype(F32)).astype(BF16)
            states[g, k] = dot_tn(w_ref[rows, vec_at], tail_x[rows, group_at])
            exits[g, k] = dot_tn(r_ref[rows, vec_at], lead_dy[rows, group_at])
            return carry

        lax.fori_loop(0, chunks, one, 0)

    def last_row(g, k, j):
        row = (k + 1) * chunk - 1
        return lead_wide[row : row + 1, columns(g, j)]

    def scan_states(g, first):
        for j in range(pairs):
            at = slice(j * LANES, (j + 1) * LANES)
            now = jnp.zeros((STATE, LANES), F32) if first else state_in[g, :, at].astype(F32)
            for k in range(chunks):
                new = states[g, k, :, at]
                states[g, k, :, at] = now
                now = last_row(g, k, j) * now + new
            states[g, chunks, :, at] = now
            state_out[g, :, at] = now.astype(BF16)

    def scan_exits(g, first):
        for j in range(pairs):
            at = slice(j * LANES, (j + 1) * LANES)
            now = jnp.zeros((STATE, LANES), F32) if first else exit_in[g, :, at].astype(F32)
            for k in reversed(range(chunks)):
                new = exits[g, k, :, at]
                exits[g, k, :, at] = now
                now = last_row(g, k, j) * now + new
            exit_out[g, :, at] = now.astype(BF16)

    def state_copy(g):
        return pltpu.make_async_remote_copy(
            src_ref=state_out.at[g],
            dst_ref=state_in.at[g],
            send_sem=s_send.at[g],
            recv_sem=s_recv.at[g],
            device_id={"ctx": jnp.minimum(ctx + 1, ctxs - 1)},
            device_id_type=MESH,
        )

    def exit_copy(g):
        return pltpu.make_async_remote_copy(
            src_ref=exit_out.at[g],
            dst_ref=exit_in.at[g],
            send_sem=e_send.at[g],
            recv_sem=e_recv.at[g],
            device_id={"ctx": jnp.maximum(ctx - 1, 0)},
            device_id_type=MESH,
        )

    def begin(g):
        @pl.when(ctx == 0)
        def _():
            scan_states(g, True)
            if ctxs > 1:
                state_copy(g).start()

        @pl.when(ctx == ctxs - 1)
        def _():
            scan_exits(g, True)
            if ctxs > 1:
                exit_copy(g).start()

    def link(g):
        @pl.when(ctx > 0)
        def _():
            state_copy(g).wait_recv()
            scan_states(g, False)

        if ctxs > 2:

            @pl.when((ctx > 0) & (ctx < ctxs - 1))
            def _():
                state_copy(g).start()

        @pl.when(ctx < ctxs - 1)
        def _():
            exit_copy(g).wait_recv()
            scan_exits(g, False)

        if ctxs > 2:

            @pl.when((ctx > 0) & (ctx < ctxs - 1))
            def _():
                exit_copy(g).start()

    def dx_copy(g, k):
        rows = pl.ds(pl.multiple_of(k * chunk, chunk), chunk)
        at = pl.ds(g * width, width)
        return pltpu.make_async_remote_copy(
            src_ref=dx.at[rows, at],
            dst_ref=up_ref.at[rows, at],
            send_sem=x_send.at[g, k],
            recv_sem=x_recv.at[g, k],
            device_id={"section": jnp.maximum(section - 1, 0)},
            device_id_type=MESH,
        )

    def vec_copy(g, k):
        return pltpu.make_async_remote_copy(
            src_ref=vec_out.at[g, k],
            dst_ref=vec_in.at[g, tp],
            send_sem=v_send.at[g, k],
            recv_sem=v_recv.at[g, tp],
            device_id={"tp": k},
            device_id_type=MESH,
        )

    def vec_arrival(g, k):
        return pltpu.make_async_remote_copy(
            src_ref=vec_out.at[g, k],
            dst_ref=vec_in.at[g, k],
            send_sem=v_send.at[g, k],
            recv_sem=v_recv.at[g, k],
            device_id={"tp": k},
            device_id_type=MESH,
        )

    def quadratic(g):
        vec_at = slice(g * STATE, (g + 1) * STATE)
        group_at = slice(g * width, (g + 1) * width)
        own = slice(g * per_group, (g + 1) * per_group)

        def one(k, carry):
            rows = pl.ds(pl.multiple_of(k * chunk, chunk), chunk)
            w, r = w_ref[rows, vec_at], r_ref[rows, vec_at]
            scores = jnp.where(causal, dot_nt(r, w), 0.0)
            da[...] = jnp.zeros_like(da)
            state, exit_ = states[g, k].astype(BF16), exits[g, k].astype(BF16)
            read_state[...] = dot_nn(r, state)
            write_exit[...] = dot_nn(w, exit_)
            edge[0:1, :] = jnp.sum(exits[g, k] * states[g, k + 1], axis=0, keepdims=True)
            for j in range(pairs):
                at = columns(g, j)
                here = slice(j * LANES, (j + 1) * LANES)
                head = g * per_group + 2 * j
                xs, dys = x_ref[rows, at], dy_ref[rows, at]
                none = jnp.zeros_like(xs)
                x_split = jnp.concatenate(
                    [jnp.where(first_half, xs, none), jnp.where(first_half, none, xs)], axis=0
                )
                dy_split = jnp.concatenate(
                    [jnp.where(first_half, dys, none), jnp.where(first_half, none, dys)], axis=0
                )
                product = dot_nt(dy_split, xs)
                weights = []
                total = da[...]
                for u in range(2):
                    one_head = head + u
                    gap = cum[rows, one_head : one_head + 1] - cum_rows[one_head : one_head + 1, rows]
                    kept = jnp.exp2(jnp.minimum(gap, 0.0)) * step_rows[one_head : one_head + 1, rows]
                    weights.append((kept * scores).astype(BF16))
                    total = total + kept * product[u * chunk : (u + 1) * chunk]
                da[...] = total
                y = dot_nn(jnp.concatenate(weights, axis=1), x_split)
                y = y + lead_wide[rows, at] * read_state[:, here]
                dxs = dot_tn(jnp.concatenate(weights, axis=0), dy_split)
                dxs = dxs + tail_wide[rows, at] * write_exit[:, here]
                x32, dy32 = xs.astype(F32), dys.astype(F32)
                column = x32 * dxs
                rest = dy32 * y - column
                high = rest.astype(BF16)
                pieces[0:chunk, here] = high
                pieces[chunk : 2 * chunk, here] = (rest - high.astype(F32)).astype(BF16)
                pieces[2 * chunk : 3 * chunk, here] = column.astype(BF16)
                edge[1:2, here] = jnp.sum(x32 * dy32, axis=0, keepdims=True)
                gain = jnp.where(
                    first_half[0:1],
                    jnp.broadcast_to(skip_ref[:, head : head + 1], (1, LANES)),
                    jnp.broadcast_to(skip_ref[:, head + 1 : head + 2], (1, LANES)),
                )
                dx[rows, at] = (dxs + gain * dy32).astype(BF16)

            @pl.when(section > 0)
            def _():
                dx_copy(g, k).start()

            inner = split(jnp.where(causal, da[...], 0.0), 2)
            dw = dot_tn(jnp.concatenate(inner, axis=0), jnp.concatenate([r, r], axis=0))
            dr = dot_nn(jnp.concatenate(inner, axis=1), jnp.concatenate([w, w], axis=0))
            dw = dw + dot_nt(tail_x[rows, group_at], exit_)
            dr = dr + dot_nt(lead_dy[rows, group_at], state)

            @pl.when(tp == k)
            def _():
                vec_in[g, k, :, 0:STATE] = dw.astype(BF16)
                vec_in[g, k, :, STATE : 2 * STATE] = dr.astype(BF16)

            @pl.when(tp != k)
            def _():
                vec_out[g, k, :, 0:STATE] = dw.astype(BF16)
                vec_out[g, k, :, STATE : 2 * STATE] = dr.astype(BF16)
                vec_copy(g, k).start()

            sums = dot_nt(gather, pieces[...])
            edges = split(edge[...], 2)
            ends = dot_nt(gather, edges[0]) + dot_nt(gather, edges[1])
            difference = sums[:, 0:chunk] + sums[:, chunk : 2 * chunk]
            decay_grad = dot_exact(difference, lower) + ends[:, 0:1]
            grad = sums[:, 2 * chunk :] * ratio[own, rows] - decay_grad * slope[own, rows]
            gdelta_ref[own, rows] = grad
            part[own, 0:1] += jnp.sum(decay_grad * decay[own, rows], axis=1, keepdims=True)
            part[own, 1:2] += jnp.sum(grad, axis=1, keepdims=True)
            part[own, 2:3] += ends[:, 1:2]
            return carry

        lax.fori_loop(0, chunks, one, 0)

    part[...] = jnp.zeros_like(part)
    edge[...] = jnp.zeros_like(edge)
    for g in range(groups):
        increments(g)
        if g == 0:
            entered()
        begin(g)
    for g in range(groups):
        link(g)
        quadratic(g)

    def part_copy(hop):
        other = lax.rem(ctx + hop, ctxs)
        return pltpu.make_async_remote_copy(
            src_ref=part,
            dst_ref=parts.at[hop - 1],
            send_sem=p_send.at[hop - 1],
            recv_sem=p_recv.at[hop - 1],
            device_id={"ctx": other},
            device_id_type=MESH,
        )

    for hop in range(1, ctxs):
        part_copy(hop).start()
    for g in range(groups):

        @pl.when(ctx < ctxs - 1)
        def _():
            state_copy(g).wait_send()

        @pl.when(ctx > 0)
        def _():
            exit_copy(g).wait_send()

        def vectors(k, carry):
            @pl.when(tp != k)
            def _():
                vec_arrival(g, k).wait_recv()
                vec_arrival(g, k).wait_send()

            return carry

        lax.fori_loop(0, tps, vectors, 0)
        for k in range(tps):
            start = (k * groups + g) * 2 * STATE
            vec_ref[:, start : start + 2 * STATE] = vec_in[g, k]
    result = part[...]
    for hop in range(1, ctxs):
        part_copy(hop).wait()
        result = result + parts[hop - 1]
    params_ref[...] = jnp.transpose(result)[0:8]
    for g in range(groups):

        def moved(k, carry):
            @pl.when(section > 0)
            def _():
                dx_copy(g, k).wait_send()

            @pl.when(section < sections - 1)
            def _():
                dx_copy(g, k).wait_recv()

            return carry

        lax.fori_loop(0, chunks, moved, 0)


def finish(sections, up_ref, gdelta_ref, vec_ref, params_ref, up_out, gdelta_out, vec_out, out):
    last = lax.axis_index("section") == sections - 1
    up_out[...] = jnp.where(last, jnp.zeros_like(up_ref[...]), up_ref[...])
    gdelta_out[...] = gdelta_ref[...]
    vec_out[...] = vec_ref[...].astype(F32)
    out[...] = params_ref[0:3]


def shards(
    sizes,
    mixer_input,
    write_vectors,
    read_vectors,
    delta_raw,
    log_rates,
    delta_bias,
    skip_gain,
    output_grad,
):
    sections, ctxs, tps = sizes
    length, heads = delta_raw.shape[1:]
    columns = mixer_input.shape[2]
    groups = write_vectors.shape[2] // STATE
    width = columns // groups
    chunk = length // tps
    dma = pltpu.SemaphoreType.DMA
    vmem = pltpu.VMEM
    scratch = [
        vmem((length, heads), F32),
        vmem((heads, length), F32),
        vmem((heads, length), F32),
        vmem((groups, 2, 2 * heads // groups, length), BF16),
        vmem((heads, length), F32),
        vmem((heads, length), F32),
        vmem((heads, length), F32),
        vmem((length, columns), F32),
        vmem((length, columns), F32),
        vmem((length, columns), BF16),
        vmem((length, columns), BF16),
        vmem((groups, tps + 1, STATE, width), F32),
        vmem((groups, tps, STATE, width), F32),
        vmem((groups, STATE, width), BF16),
        vmem((groups, STATE, width), BF16),
        vmem((groups, STATE, width), BF16),
        vmem((groups, STATE, width), BF16),
        vmem((chunk, width), F32),
        vmem((chunk, width), F32),
        vmem((chunk, chunk), F32),
        vmem((3 * chunk, width), BF16),
        vmem((8, width), F32),
        vmem((length, columns), BF16),
        vmem((groups, tps, chunk, 2 * STATE), BF16),
        vmem((groups, tps, chunk, 2 * STATE), BF16),
        vmem((heads, LANES), F32),
        vmem((max(ctxs - 1, 1), heads, LANES), F32),
        dma((groups,)),
        dma((groups,)),
        dma((groups,)),
        dma((groups,)),
        dma((groups, tps)),
        dma((groups, tps)),
        dma((groups, tps)),
        dma((groups, tps)),
        dma((max(ctxs - 1, 1),)),
        dma((max(ctxs - 1, 1),)),
    ]
    whole = pl.BlockSpec(memory_space=pltpu.VMEM)
    upstream, grad_delta, vectors, params = pl.pallas_call(
        functools.partial(kernel, sizes),
        out_shape=(
            jax.ShapeDtypeStruct((length, columns), BF16),
            jax.ShapeDtypeStruct((heads, length), F32),
            jax.ShapeDtypeStruct((chunk, groups * tps * 2 * STATE), BF16),
            jax.ShapeDtypeStruct((8, heads), F32),
        ),
        in_specs=[whole] * 8,
        out_specs=(pl.BlockSpec(memory_space=pl.ANY), whole, whole, whole),
        scratch_shapes=scratch,
        compiler_params=pltpu.CompilerParams(
            collective_id=0, has_side_effects=True, vmem_limit_bytes=56 * 1024 * 1024
        ),
    )(
        mixer_input[0],
        write_vectors[0],
        read_vectors[0],
        delta_raw[0].T,
        log_rates,
        delta_bias,
        skip_gain,
        output_grad[0],
    )
    steps = 4
    rows, across = length // steps, vectors.shape[1] // steps
    specs = [
        pl.BlockSpec((rows, columns), lambda i: (i, 0)),
        pl.BlockSpec((heads, length), lambda i: (0, 0)),
        pl.BlockSpec((chunk, across), lambda i: (0, i)),
    ]
    upstream, grad_delta, vectors, params = pl.pallas_call(
        functools.partial(finish, sections),
        grid=(steps,),
        out_shape=(
            jax.ShapeDtypeStruct((length, columns), BF16),
            jax.ShapeDtypeStruct((heads, length), F32),
            jax.ShapeDtypeStruct(vectors.shape, F32),
            jax.ShapeDtypeStruct((3, heads), F32),
        ),
        in_specs=specs + [pl.BlockSpec((8, heads), lambda i: (0, 0))],
        out_specs=tuple(specs + [pl.BlockSpec((3, heads), lambda i: (0, 0))]),
    )(upstream, grad_delta, vectors, params)
    return (upstream[None], grad_delta.T[None], vectors[None], params[None])


def solution(mesh):
    sizes = tuple(mesh.shape[a] for a in ("section", "ctx", "tp"))
    in_specs = (
        P("section", "ctx", "tp"),
        P("section", "ctx", "tp"),
        P("section", "ctx", "tp"),
        P("section", "ctx", "tp"),
        P("section", "tp"),
        P("section", "tp"),
        P("section", "tp"),
        P("section", "ctx", "tp"),
    )
    out_specs = (
        P("section", "ctx", "tp"),
        P("section", "ctx", "tp"),
        P("section", ("ctx", "tp"), None),
        P("section", None, "tp"),
    )
    return jax.shard_map(
        functools.partial(shards, sizes),
        mesh=mesh,
        in_specs=in_specs,
        out_specs=out_specs,
        check_vma=False,
    )
```

```python
import functools
import math

import jax
import jax.numpy as jnp
from jax import lax
from jax.experimental import pallas as pl
from jax.experimental.pallas import tpu as pltpu
from jax.sharding import PartitionSpec as P

HEADDIM = 64
STATE = 128
LANES = 128
LOG2E = math.log2(math.e)
MESH = pl.DeviceIdType.MESH
HIGHEST = lax.Precision.HIGHEST
F32 = jnp.float32
BF16 = jnp.bfloat16


def dot_nn(a, b, precision=None):
    return lax.dot_general(
        a, b, (((1,), (0,)), ((), ())), precision=precision, preferred_element_type=F32
    )


def dot_nt(a, b):
    return lax.dot_general(a, b, (((1,), (1,)), ((), ())), preferred_element_type=F32)


def dot_tn(a, b):
    return lax.dot_general(a, b, (((0,), (0,)), ((), ())), preferred_element_type=F32)


def split(a, parts):
    out = []
    for _ in range(parts):
        out.append(a.astype(BF16))
        a = a - out[-1].astype(F32)
    return out


def dot_exact(a, b):
    rows = a.shape[0]
    terms = dot_nn(jnp.concatenate(split(a, 3), axis=0), b)
    return terms[0:rows] + terms[rows : 2 * rows] + terms[2 * rows : 3 * rows]


def kernel(
    sizes,
    x_hbm,
    w_ref,
    r_ref,
    delta_ref,
    rates_ref,
    bias_ref,
    skip_ref,
    dy_hbm,
    up_ref,
    gdelta_ref,
    vec_ref,
    params_ref,
    x_ref,
    dy_ref,
    cum,
    cum_rows,
    step_rows,
    scales,
    decay,
    ratio,
    slope,
    lead_wide,
    tail_wide,
    lead_dy,
    tail_x,
    states,
    exits,
    state_in,
    state_out,
    exit_in,
    exit_out,
    read_state,
    write_exit,
    da,
    pieces,
    edge,
    dx,
    vec_out,
    vec_in,
    part,
    parts,
    loads,
    s_send,
    s_recv,
    e_send,
    e_recv,
    x_send,
    x_recv,
    v_send,
    v_recv,
    p_send,
    p_recv,
):
    sections, ctxs, tps = sizes
    section, ctx, tp = (lax.axis_index(a) for a in ("section", "ctx", "tp"))
    heads, length = delta_ref.shape
    groups = w_ref.shape[1] // STATE
    per_group = heads // groups
    width = per_group * HEADDIM
    chunk = length // tps
    chunks = tps
    pairs = width // LANES

    def load(g):
        at = pl.ds(g * width, width)
        return (
            pltpu.make_async_copy(x_hbm.at[:, at], x_ref.at[:, at], loads.at[0, g]),
            pltpu.make_async_copy(dy_hbm.at[:, at], dy_ref.at[:, at], loads.at[1, g]),
        )

    for g in range(groups):
        for copy in load(g):
            copy.start()

    barrier = pltpu.get_barrier_semaphore()
    for hop in range(1, ctxs):
        pl.semaphore_signal(
            barrier, inc=1, device_id={"ctx": lax.rem(ctx + hop, ctxs)}, device_id_type=MESH
        )
    for hop in range(1, tps):
        pl.semaphore_signal(
            barrier, inc=1, device_id={"tp": lax.rem(tp + hop, tps)}, device_id_type=MESH
        )

    @pl.when(section > 0)
    def _():
        pl.semaphore_signal(barrier, inc=1, device_id={"section": section - 1}, device_id_type=MESH)

    @pl.when(section < sections - 1)
    def _():
        pl.semaphore_signal(barrier, inc=1, device_id={"section": section + 1}, device_id_type=MESH)

    up_to = lax.broadcasted_iota(jnp.int32, (chunk, chunk), 0)
    from_ = lax.broadcasted_iota(jnp.int32, (chunk, chunk), 1)
    causal = up_to >= from_
    lower = causal.astype(BF16)
    upper = (up_to <= from_).astype(BF16)
    first_half = lax.broadcasted_iota(jnp.int32, (chunk, LANES), 1) < HEADDIM
    rate = jnp.transpose(jnp.broadcast_to(jnp.exp(rates_ref[...]), (chunk, heads)))
    bias = jnp.transpose(jnp.broadcast_to(bias_ref[...], (chunk, heads)))
    for k in range(chunks):
        rows = slice(k * chunk, (k + 1) * chunk)
        z = delta_ref[:, rows] + bias
        small = jnp.exp(-jnp.abs(z))
        step = jnp.maximum(z, 0.0) + jnp.log1p(small)
        sig = jnp.where(z >= 0, 1.0, small) / (1.0 + small)
        dec = -step * rate
        decay[:, rows] = dec
        ratio[:, rows] = jnp.where(step > 1e-37, sig / jnp.maximum(step, 1e-37), 1.0)
        slope[:, rows] = sig * rate
        run = dot_exact(dec * LOG2E, upper)
        cum[rows, :] = jnp.transpose(run)
        cum_rows[:, rows] = run
        step_rows[:, rows] = step
        lead = split(jnp.exp2(run), 2)
        tail = split(jnp.exp2(run[:, chunk - 1 : chunk] - run) * step, 2)
        for g in range(groups):
            own = slice(g * per_group, (g + 1) * per_group)
            scales[g, 0, :, rows] = jnp.concatenate([lead[0][own], lead[1][own]], axis=0)
            scales[g, 1, :, rows] = jnp.concatenate([tail[0][own], tail[1][own]], axis=0)
    head_of = lax.broadcasted_iota(jnp.int32, (2 * per_group, width), 1) // HEADDIM
    row_of = lax.broadcasted_iota(jnp.int32, (2 * per_group, width), 0)
    both = (head_of == lax.rem(row_of, per_group)).astype(BF16)
    gather = both[0:per_group]

    def entered():
        peers = (ctxs - 1) + (tps - 1)
        peers = peers + jnp.where(section > 0, 1, 0) + jnp.where(section < sections - 1, 1, 0)
        pl.semaphore_wait(barrier, peers)

    def columns(g, j):
        start = g * width + j * LANES
        return slice(start, start + LANES)

    def increments(g):
        for copy in load(g):
            copy.wait()

        def one(k, carry):
            rows = pl.ds(pl.multiple_of(k * chunk, chunk), chunk)
            group_at = slice(g * width, (g + 1) * width)
            vec_at = slice(g * STATE, (g + 1) * STATE)
            lead_all = dot_tn(scales[g, 0, :, rows], both)
            tail_all = dot_tn(scales[g, 1, :, rows], both)
            lead_wide[rows, group_at] = lead_all
            tail_wide[rows, group_at] = tail_all
            w, r = w_ref[rows, vec_at], r_ref[rows, vec_at]
            later = split(tail_all * x_ref[rows, group_at].astype(F32), 2)
            tail_x[rows, group_at] = later[0]
            states[g, k] = dot_tn(jnp.concatenate([w, w], axis=0), jnp.concatenate(later, axis=0))
            later = split(lead_all * dy_ref[rows, group_at].astype(F32), 2)
            lead_dy[rows, group_at] = later[0]
            exits[g, k] = dot_tn(jnp.concatenate([r, r], axis=0), jnp.concatenate(later, axis=0))
            return carry

        lax.fori_loop(0, chunks, one, 0)

    def last_row(g, k, j):
        row = (k + 1) * chunk - 1
        return lead_wide[row : row + 1, columns(g, j)]

    def scan_states(g, first):
        for j in range(pairs):
            at = slice(j * LANES, (j + 1) * LANES)
            now = jnp.zeros((STATE, LANES), F32) if first else state_in[g, :, at].astype(F32)
            for k in range(chunks):
                new = states[g, k, :, at]
                states[g, k, :, at] = now
                now = last_row(g, k, j) * now + new
            states[g, chunks, :, at] = now
            state_out[g, :, at] = now.astype(BF16)

    def scan_exits(g, first):
        for j in range(pairs):
            at = slice(j * LANES, (j + 1) * LANES)
            now = jnp.zeros((STATE, LANES), F32) if first else exit_in[g, :, at].astype(F32)
            for k in reversed(range(chunks)):
                new = exits[g, k, :, at]
                exits[g, k, :, at] = now
                now = last_row(g, k, j) * now + new
            exit_out[g, :, at] = now.astype(BF16)

    def state_copy(g):
        return pltpu.make_async_remote_copy(
            src_ref=state_out.at[g],
            dst_ref=state_in.at[g],
            send_sem=s_send.at[g],
            recv_sem=s_recv.at[g],
            device_id={"ctx": jnp.minimum(ctx + 1, ctxs - 1)},
            device_id_type=MESH,
        )

    def exit_copy(g):
        return pltpu.make_async_remote_copy(
            src_ref=exit_out.at[g],
            dst_ref=exit_in.at[g],
            send_sem=e_send.at[g],
            recv_sem=e_recv.at[g],
            device_id={"ctx": jnp.maximum(ctx - 1, 0)},
            device_id_type=MESH,
        )

    def begin(g):
        @pl.when(ctx == 0)
        def _():
            scan_states(g, True)
            if ctxs > 1:
                state_copy(g).start()

        @pl.when(ctx == ctxs - 1)
        def _():
            scan_exits(g, True)
            if ctxs > 1:
                exit_copy(g).start()

    def link(g):
        @pl.when(ctx > 0)
        def _():
            state_copy(g).wait_recv()
            scan_states(g, False)

        if ctxs > 2:

            @pl.when((ctx > 0) & (ctx < ctxs - 1))
            def _():
                state_copy(g).start()

        @pl.when(ctx < ctxs - 1)
        def _():
            exit_copy(g).wait_recv()
            scan_exits(g, False)

        if ctxs > 2:

            @pl.when((ctx > 0) & (ctx < ctxs - 1))
            def _():
                exit_copy(g).start()

    def dx_copy(g, k, half):
        rows = pl.ds(pl.multiple_of(k * chunk, chunk), chunk)
        at = pl.ds(g * width + half * (width // 2), width // 2)
        return pltpu.make_async_remote_copy(
            src_ref=dx.at[rows, at],
            dst_ref=up_ref.at[rows, at],
            send_sem=x_send.at[g, k, half],
            recv_sem=x_recv.at[g, k, half],
            device_id={"section": jnp.maximum(section - 1, 0)},
            device_id_type=MESH,
        )

    def vec_copy(g, k):
        return pltpu.make_async_remote_copy(
            src_ref=vec_out.at[g, k],
            dst_ref=vec_in.at[g, tp],
            send_sem=v_send.at[g, k],
            recv_sem=v_recv.at[g, tp],
            device_id={"tp": k},
            device_id_type=MESH,
        )

    def vec_arrival(g, k):
        return pltpu.make_async_remote_copy(
            src_ref=vec_out.at[g, k],
            dst_ref=vec_in.at[g, k],
            send_sem=v_send.at[g, k],
            recv_sem=v_recv.at[g, k],
            device_id={"tp": k},
            device_id_type=MESH,
        )

    def quadratic(g):
        vec_at = slice(g * STATE, (g + 1) * STATE)
        group_at = slice(g * width, (g + 1) * width)
        own = slice(g * per_group, (g + 1) * per_group)

        def one(k, carry):
            rows = pl.ds(pl.multiple_of(k * chunk, chunk), chunk)
            w, r = w_ref[rows, vec_at], r_ref[rows, vec_at]
            scores = jnp.where(causal, dot_nt(r, w), 0.0)
            da[...] = jnp.zeros_like(da)
            state, exit_ = split(states[g, k], 2), split(exits[g, k], 2)
            read_state[...] = dot_nn(
                jnp.concatenate([r, r], axis=1), jnp.concatenate(state, axis=0)
            )
            write_exit[...] = dot_nn(
                jnp.concatenate([w, w], axis=1), jnp.concatenate(exit_, axis=0)
            )
            edge[0:1, :] = jnp.sum(exits[g, k] * states[g, k + 1], axis=0, keepdims=True)
            for j in range(pairs):
                at = columns(g, j)
                here = slice(j * LANES, (j + 1) * LANES)
                head = g * per_group + 2 * j
                xs, dys = x_ref[rows, at], dy_ref[rows, at]
                none = jnp.zeros_like(xs)
                x_split = jnp.concatenate(
                    [jnp.where(first_half, xs, none), jnp.where(first_half, none, xs)], axis=0
                )
                dy_split = jnp.concatenate(
                    [jnp.where(first_half, dys, none), jnp.where(first_half, none, dys)], axis=0
                )
                product = dot_nt(dy_split, xs)
                weights = []
                total = da[...]
                for u in range(2):
                    one_head = head + u
                    gap = cum[rows, one_head : one_head + 1] - cum_rows[one_head : one_head + 1, rows]
                    kept = jnp.exp2(jnp.minimum(gap, 0.0)) * step_rows[one_head : one_head + 1, rows]
                    weights.append((kept * scores).astype(BF16))
                    total = total + kept * product[u * chunk : (u + 1) * chunk]
                da[...] = total
                y = dot_nn(jnp.concatenate(weights, axis=1), x_split)
                y = y + lead_wide[rows, at] * read_state[:, here]
                dxs = dot_tn(jnp.concatenate(weights, axis=0), dy_split)
                dxs = dxs + tail_wide[rows, at] * write_exit[:, here]
                x32, dy32 = xs.astype(F32), dys.astype(F32)
                column = x32 * dxs
                rest = dy32 * y - column
                high = rest.astype(BF16)
                pieces[0:chunk, here] = high
                pieces[chunk : 2 * chunk, here] = (rest - high.astype(F32)).astype(BF16)
                high = column.astype(BF16)
                pieces[2 * chunk : 3 * chunk, here] = high
                pieces[3 * chunk : 4 * chunk, here] = (column - high.astype(F32)).astype(BF16)
                edge[1:2, here] = jnp.sum(x32 * dy32, axis=0, keepdims=True)
                gain = jnp.where(
                    first_half[0:1],
                    jnp.broadcast_to(skip_ref[:, head : head + 1], (1, LANES)),
                    jnp.broadcast_to(skip_ref[:, head + 1 : head + 2], (1, LANES)),
                )
                dx[rows, at] = (dxs + gain * dy32).astype(BF16)
                if (j + 1) % (pairs // 2) == 0:

                    @pl.when(section > 0)
                    def _(half=j // (pairs // 2)):
                        dx_copy(g, k, half).start()


            inner = split(jnp.where(causal, da[...], 0.0), 2)
            dw = dot_tn(jnp.concatenate(inner, axis=0), jnp.concatenate([r, r], axis=0))
            dr = dot_nn(jnp.concatenate(inner, axis=1), jnp.concatenate([w, w], axis=0))
            for i in range(2):
                dw = dw + dot_nt(tail_x[rows, group_at], exit_[i])
                dr = dr + dot_nt(lead_dy[rows, group_at], state[i])

            @pl.when(tp == k)
            def _():
                vec_in[g, k, :, 0:STATE] = dw.astype(BF16)
                vec_in[g, k, :, STATE : 2 * STATE] = dr.astype(BF16)

            @pl.when(tp != k)
            def _():
                vec_out[g, k, :, 0:STATE] = dw.astype(BF16)
                vec_out[g, k, :, STATE : 2 * STATE] = dr.astype(BF16)
                vec_copy(g, k).start()

            sums = dot_nt(gather, pieces[...])
            edges = split(edge[...], 2)
            ends = dot_nt(gather, edges[0]) + dot_nt(gather, edges[1])
            difference = sums[:, 0:chunk] + sums[:, chunk : 2 * chunk]
            decay_grad = dot_exact(difference, lower) + ends[:, 0:1]
            direct = sums[:, 2 * chunk : 3 * chunk] + sums[:, 3 * chunk :]
            grad = direct * ratio[own, rows] - decay_grad * slope[own, rows]
            gdelta_ref[own, rows] = grad
            part[own, 0:1] += jnp.sum(decay_grad * decay[own, rows], axis=1, keepdims=True)
            part[own, 1:2] += jnp.sum(grad, axis=1, keepdims=True)
            part[own, 2:3] += ends[:, 1:2]
            return carry

        lax.fori_loop(0, chunks, one, 0)

    part[...] = jnp.zeros_like(part)
    edge[...] = jnp.zeros_like(edge)
    early = lax.rem(section, 2) == 0
    for g in range(groups):
        increments(g)
        if g == 0:
            entered()

            @pl.when(early)
            def _():
                begin(0)

        else:
            if g == 1:

                @pl.when(jnp.logical_not(early))
                def _():
                    begin(0)

            begin(g)
    if groups == 1:

        @pl.when(jnp.logical_not(early))
        def _():
            begin(0)

    for g in range(groups):
        link(g)
        quadratic(g)

    def part_copy(hop):
        other = lax.rem(ctx + hop, ctxs)
        return pltpu.make_async_remote_copy(
            src_ref=part,
            dst_ref=parts.at[hop - 1],
            send_sem=p_send.at[hop - 1],
            recv_sem=p_recv.at[hop - 1],
            device_id={"ctx": other},
            device_id_type=MESH,
        )

    for hop in range(1, ctxs):
        part_copy(hop).start()
    for g in range(groups):

        @pl.when(ctx < ctxs - 1)
        def _():
            state_copy(g).wait_send()

        @pl.when(ctx > 0)
        def _():
            exit_copy(g).wait_send()

        def vectors(k, carry):
            @pl.when(tp != k)
            def _():
                vec_arrival(g, k).wait_recv()
                vec_arrival(g, k).wait_send()

            return carry

        lax.fori_loop(0, tps, vectors, 0)
        for k in range(tps):
            start = (k * groups + g) * 2 * STATE
            vec_ref[:, start : start + 2 * STATE] = vec_in[g, k]
    result = part[...]
    for hop in range(1, ctxs):
        part_copy(hop).wait()
        result = result + parts[hop - 1]
    params_ref[...] = jnp.transpose(result)[0:8]
    for g in range(groups):

        def moved(k, carry):
            @pl.when(section > 0)
            def _():
                for half in range(2):
                    dx_copy(g, k, half).wait_send()

            @pl.when(section < sections - 1)
            def _():
                for half in range(2):
                    dx_copy(g, k, half).wait_recv()

            return carry

        lax.fori_loop(0, chunks, moved, 0)


def finish(sections, up_ref, gdelta_ref, vec_ref, params_ref, up_out, gdelta_out, vec_out, out):
    last = lax.axis_index("section") == sections - 1
    up_out[...] = jnp.where(last, jnp.zeros_like(up_ref[...]), up_ref[...])
    gdelta_out[...] = gdelta_ref[...]
    vec_out[...] = vec_ref[...].astype(F32)
    for i in range(3):
        out[i] = params_ref[i : i + 1]


def shards(
    sizes,
    mixer_input,
    write_vectors,
    read_vectors,
    delta_raw,
    log_rates,
    delta_bias,
    skip_gain,
    output_grad,
):
    sections, ctxs, tps = sizes
    length, heads = delta_raw.shape[1:]
    columns = mixer_input.shape[2]
    groups = write_vectors.shape[2] // STATE
    width = columns // groups
    chunk = length // tps
    dma = pltpu.SemaphoreType.DMA
    vmem = pltpu.VMEM
    scratch = [
        vmem((length, columns), BF16),
        vmem((length, columns), BF16),
        vmem((length, heads), F32),
        vmem((heads, length), F32),
        vmem((heads, length), F32),
        vmem((groups, 2, 2 * heads // groups, length), BF16),
        vmem((heads, length), F32),
        vmem((heads, length), F32),
        vmem((heads, length), F32),
        vmem((length, columns), F32),
        vmem((length, columns), F32),
        vmem((length, columns), BF16),
        vmem((length, columns), BF16),
        vmem((groups, tps + 1, STATE, width), F32),
        vmem((groups, tps, STATE, width), F32),
        vmem((groups, STATE, width), BF16),
        vmem((groups, STATE, width), BF16),
        vmem((groups, STATE, width), BF16),
        vmem((groups, STATE, width), BF16),
        vmem((chunk, width), F32),
        vmem((chunk, width), F32),
        vmem((chunk, chunk), F32),
        vmem((4 * chunk, width), BF16),
        vmem((8, width), F32),
        vmem((length, columns), BF16),
        vmem((groups, tps, chunk, 2 * STATE), BF16),
        vmem((groups, tps, chunk, 2 * STATE), BF16),
        vmem((heads, LANES), F32),
        vmem((max(ctxs - 1, 1), heads, LANES), F32),
        dma((2, groups)),
        dma((groups,)),
        dma((groups,)),
        dma((groups,)),
        dma((groups,)),
        dma((groups, tps, 2)),
        dma((groups, tps, 2)),
        dma((groups, tps)),
        dma((groups, tps)),
        dma((max(ctxs - 1, 1),)),
        dma((max(ctxs - 1, 1),)),
    ]
    whole = pl.BlockSpec(memory_space=pltpu.VMEM)
    far = pl.BlockSpec(memory_space=pl.ANY)
    upstream, grad_delta, vectors, params = pl.pallas_call(
        functools.partial(kernel, sizes),
        out_shape=(
            jax.ShapeDtypeStruct((length, columns), BF16),
            jax.ShapeDtypeStruct((heads, length), F32),
            jax.ShapeDtypeStruct((chunk, groups * tps * 2 * STATE), BF16),
            jax.ShapeDtypeStruct((8, heads), F32),
        ),
        in_specs=[far] + [whole] * 6 + [far],
        out_specs=(far, whole, whole, whole),
        scratch_shapes=scratch,
        compiler_params=pltpu.CompilerParams(
            collective_id=0, has_side_effects=True, vmem_limit_bytes=56 * 1024 * 1024
        ),
    )(
        mixer_input[0],
        write_vectors[0],
        read_vectors[0],
        delta_raw[0].T,
        log_rates,
        delta_bias,
        skip_gain,
        output_grad[0],
    )
    steps = 4
    rows, across = length // steps, vectors.shape[1] // steps
    specs = [
        pl.BlockSpec((rows, columns), lambda i: (i, 0)),
        pl.BlockSpec((heads, length), lambda i: (0, 0)),
        pl.BlockSpec((chunk, across), lambda i: (0, i)),
    ]
    upstream, grad_delta, vectors, params = pl.pallas_call(
        functools.partial(finish, sections),
        grid=(steps,),
        out_shape=(
            jax.ShapeDtypeStruct((length, columns), BF16),
            jax.ShapeDtypeStruct((heads, length), F32),
            jax.ShapeDtypeStruct(vectors.shape, F32),
            jax.ShapeDtypeStruct((3, 1, heads), F32),
        ),
        in_specs=specs + [pl.BlockSpec((8, heads), lambda i: (0, 0))],
        out_specs=tuple(specs + [pl.BlockSpec((3, 1, heads), lambda i: (0, 0, 0))]),
    )(upstream, grad_delta, vectors, params)
    return (upstream[None], grad_delta.T[None], vectors[None], params.transpose(1, 0, 2))


def solution(mesh):
    sizes = tuple(mesh.shape[a] for a in ("section", "ctx", "tp"))
    in_specs = (
        P("section", "ctx", "tp"),
        P("section", "ctx", "tp"),
        P("section", "ctx", "tp"),
        P("section", "ctx", "tp"),
        P("section", "tp"),
        P("section", "tp"),
        P("section", "tp"),
        P("section", "ctx", "tp"),
    )
    out_specs = (
        P("section", "ctx", "tp"),
        P("section", "ctx", "tp"),
        P("section", ("ctx", "tp"), None),
        P("section", None, "tp"),
    )
    return jax.shard_map(
        functools.partial(shards, sizes),
        mesh=mesh,
        in_specs=in_specs,
        out_specs=out_specs,
        check_vma=False,
    )
```
